32 devices in a mesh: dp: 2 (over x), expert: 16 (over z, y, core).
Axes of the slice: x: 2, y: 2, z: 4, core: 2. Of those that a mesh axis runs over, the one named last changes fastest.
Arguments:
- tokens: bfloat16 [2048, 2048], P('expert', 'dp'), may hold values from -6 to 6
- expert_ids: int32 [2048, 8], P('expert'), may hold values from 0 to 15, all different within a row; in each aligned block of 128 rows (0 to 127, 128 to 255, ...) at most 96 rows name the same one
- chosen_probs: float32 [2048, 8], P('expert'), may hold values from 0.05 to 1
- gate_weight: bfloat16 [16, 1536, 2048], P('expert', 'dp'), may hold values from -0.125 to 0.125
- up_weight: bfloat16 [16, 1536, 2048], P('expert', 'dp'), may hold values from -0.125 to 0.125
- down_weight: bfloat16 [16, 1536, 2048], P('expert', 'dp'), may hold values from -0.15625 to 0.15625
Outputs:
- mixed: bfloat16 [2048, 2048], P('expert', 'dp')
The draws below stay inside these ranges and needn't reach their ends.
Inputs may be any that keep to these rules, and one draw needn't show every extreme that they name: `expert_ids`: each row names 8 different experts; the 128 rows of one device name each expert at most 96 times, a bound that some block reaches.
All inputs are finite; a program needn't handle non-finite values.
Results may differ from the reference program's by a relative error of at most 0.0058.
Values may be sent and summed in bfloat16 or wider, within the bound.
No kernel may reach another device: no remote copies, remote signals or barrier semaphores. Data moves between devices by JAX's collectives and lax.ppermute only.
A program may use at most 128 MiB of HBM per device.

```python
import math
import jax
import jax.numpy as jnp
import numpy as np
from jax import lax

D = 2048
FF = 1536
TOP = 8
TOK_DEV = 128
EXPERTS = 16
CAP = 96
TOKENS = 2048
N_DP = 2
N_EXPERT = 16


def steps_of(rng, dims, shards, low, top_value):
    gain = 1.0
    for axis_at, parts in shards:
        heights = jax.random.uniform(jax.random.fold_in(jax.random.fold_in(rng, 6), axis_at), (parts,), jnp.float32, low / len(shards), top_value / len(shards))
        gain = gain * jnp.repeat(jnp.exp(heights), dims[axis_at] // parts).reshape((-1,) + (1,) * (len(dims) - 1 - axis_at))
    return gain


def assign_block(stream_key, own, number, rows, count, top, most, skew):
    order = jax.random.permutation(stream_key, count)
    heavy_load, common = load_shares(count, rows * top, most, skew, True), load_shares(count, rows * top, most, skew, False)
    places = jnp.arange(count)

    def named(lengths, offset_by):
        used = int((lengths > 0).sum())
        fixed = max(1, used // 4)
        moved = fixed + (places - fixed + offset_by * (used - fixed)) % max(1, count - fixed)
        return jnp.zeros((count,), jnp.int32).at[order[jnp.where(places < fixed, places, moved)]].set(jnp.asarray(lengths, jnp.int32))

    lengths = jnp.where(number % 4 == 0, named(heavy_load, number // 4), named(common, number - number // 4 - 1))
    mixed = jax.random.permutation(jax.random.fold_in(own, 3), count)
    giver, receiver = mixed[0:count // 2 * 2:2], mixed[1:count // 2 * 2:2]
    room = jnp.minimum(lengths[giver] - 1, most - lengths[receiver]) // 2
    room = jnp.where((giver == order[0]) | (receiver == order[0]) | (lengths[receiver] == 0), 0, jnp.maximum(room, 0))
    moved = jax.random.randint(jax.random.fold_in(own, 4), (count // 2,), 0, 1 << 20) % (room + 1)
    lengths = lengths.at[giver].add(-moved).at[receiver].add(moved)
    items = jnp.searchsorted(jnp.cumsum(lengths), jnp.arange(rows * top), side="right").astype(jnp.int32)
    listing = items.reshape(top, rows).T
    listing = listing[jax.random.permutation(jax.random.fold_in(own, 1), rows)]
    offset_by = jax.random.randint(jax.random.fold_in(own, 2), (rows, 1), 0, top)
    return jnp.take_along_axis(listing, (jnp.arange(top)[None, :] + offset_by) % top, axis=1)


def load_shares(amount, total, bound, slope, full):
    weights = [(1 << 20) // math.isqrt(standing ** slope) + 1 for standing in range(1, amount + 1)]
    largest = bound if full else min(bound, max(-(-total // amount), total * weights[0] // sum(weights)))
    least = 1 if total - largest >= amount - 1 else 0
    counts, spare = [largest] + [least] * (amount - 1), total - largest - least * (amount - 1)
    while spare > 0:
        free = [i for i in range(1, amount) if counts[i] < largest] or [i for i in range(1, amount) if counts[i] < bound]
        pool, budget = sum([weights[i] for i in free]), spare
        for i in free:
            extra = min(bound - counts[i], max(1, budget * weights[i] // pool), spare)
            counts[i] = counts[i] + extra
            spare = spare - extra
    return np.array(counts)


def normal_values(own_key, shape, scale, reach, shards=(), kind=jnp.bfloat16):
    drawn = jax.random.normal(own_key, shape, jnp.float32) * scale
    if len(shards) > 0:
        drawn = steps_of(own_key, shape, shards, -0.22, 0.18) * drawn
    return jnp.clip(drawn, min=-reach, max=reach).astype(kind)


def setup_inputs(seed: int = 0) -> dict:
    keys = jax.random.split(jax.random.key(seed), 7)
    tokens = normal_values(keys[0], (TOKENS, D), 1.0, 6.0, ((0, 16), (1, 2)))
    expert_ids_keys = jax.random.split(jax.random.fold_in(keys[1], 1), TOKENS // TOK_DEV)
    expert_ids_turns = jax.random.permutation(jax.random.fold_in(keys[1], 3), TOKENS // TOK_DEV)
    expert_ids = jax.vmap(lambda own, number: assign_block(jax.random.fold_in(keys[1], 2), own, number, TOK_DEV, EXPERTS, TOP, CAP, 2))(expert_ids_keys, expert_ids_turns).reshape((TOKENS, TOP))
    chosen_probs = jnp.clip(jnp.exp(math.log(1.0) - 2.9957323 * jax.random.uniform(keys[2], (TOKENS, TOP), jnp.float32) ** steps_of(keys[2], (TOKENS, TOP), ((0, 16),), -0.2, 0.2)), 0.05, 1.0)
    gate_weight = normal_values(keys[3], (EXPERTS, FF, D), D ** -0.5, 0.125, ((0, 16), (1, 2)))
    up_weight = normal_values(keys[4], (EXPERTS, FF, D), D ** -0.5, 0.125, ((0, 16), (1, 2)))
    down_weight = normal_values(keys[5], (EXPERTS, FF, D), FF ** -0.5, 0.15625, ((0, 16), (1, 2)))
    return {"tokens": tokens, "expert_ids": expert_ids, "chosen_probs": chosen_probs, "gate_weight": gate_weight, "up_weight": up_weight, "down_weight": down_weight}


def reference(tokens, expert_ids, chosen_probs, gate_weight, up_weight, down_weight):
    route = chosen_probs / jnp.sum(chosen_probs, axis=1, keepdims=True)
    ntok = tokens.shape[0]
    width = tokens.shape[1]
    flat = expert_ids.reshape(-1).astype(jnp.int32)
    count = ntok * TOP
    onehot = (flat[:, None] == jnp.arange(EXPERTS, dtype=jnp.int32)[None, :]).astype(jnp.int32)
    blocked = onehot.reshape(N_EXPERT, TOK_DEV * TOP, EXPERTS)
    ranks = (jnp.cumsum(blocked, axis=1) - 1).reshape(count, EXPERTS)
    slot = jnp.sum(onehot * ranks, axis=1).astype(jnp.int32)
    owner = (jnp.arange(count, dtype=jnp.int32) // (TOK_DEV * TOP)).astype(jnp.int32)
    place = ((flat * N_EXPERT + owner) * CAP + slot).astype(jnp.int32)
    table = jnp.zeros((EXPERTS * N_EXPERT * CAP,), jnp.int32).at[place].set(jnp.arange(count, dtype=jnp.int32) + 1)
    table = table.reshape(EXPERTS, N_EXPERT * CAP)
    tok_of = jnp.concatenate([jnp.zeros((1,), jnp.int32), (jnp.arange(count, dtype=jnp.int32) // TOP + 1).astype(jnp.int32)])
    weight_of = jnp.concatenate([jnp.zeros((1,), jnp.float32), route.reshape(-1).astype(jnp.float32)])
    padded = jnp.concatenate([jnp.zeros((1, width), tokens.dtype), tokens], axis=0)
    block = FF // N_DP

    def one_expert(total, items):
        gate_w, up_w, down_w, entries = items
        tok_index = tok_of[entries]
        weights = weight_of[entries]
        rows = padded[tok_index]
        gate = jnp.dot(rows, gate_w.T, preferred_element_type=jnp.float32)
        up = jnp.dot(rows, up_w.T, preferred_element_type=jnp.float32)
        hidden = (jax.nn.silu(gate) * up).astype(jnp.bfloat16)
        for piece in range(N_DP):
            part = jnp.dot(hidden[:, piece * block:(piece + 1) * block], down_w[piece * block:(piece + 1) * block], preferred_element_type=jnp.float32).astype(jnp.bfloat16)
            total = total.at[tok_index].add(part.astype(jnp.float32) * weights[:, None])
        return total, None

    start = jnp.zeros((ntok + 1, width), jnp.float32)
    total, _ = lax.scan(one_expert, start, (gate_weight, up_weight, down_weight, table))
    return total[1:].astype(jnp.bfloat16)
```

```python
import jax
import jax.numpy as jnp
from jax import lax
from jax.experimental import pallas as pl
from jax.experimental.pallas import tpu as pltpu
from jax.sharding import PartitionSpec as P

CHUNKS = 2


def exchange(tokens, expert_ids, chosen_probs, gate_weight, up_weight, down_weight):
    n_experts = lax.axis_size("expert")
    tok_rows = expert_ids.shape[0]
    top_count = expert_ids.shape[1]
    capacity = min(
        tok_rows, max(2, (3 * tok_rows * top_count + 2 * n_experts - 1) // (2 * n_experts))
    )
    route = chosen_probs / jnp.sum(chosen_probs, axis=1, keepdims=True)
    flat = expert_ids.reshape(-1)
    onehot = (flat[:, None] == jnp.arange(n_experts, dtype=jnp.int32)[None, :]).astype(jnp.int32)
    slot = jnp.sum(onehot * (jnp.cumsum(onehot, axis=0) - 1), axis=1)
    place = flat * capacity + slot
    tok_index = jnp.arange(tok_rows * top_count, dtype=jnp.int32) // top_count
    source = lax.all_gather(tokens, "dp", axis=1, tiled=True)
    columns_now = source.shape[1]
    buffer = (
        jnp.zeros((n_experts * capacity, columns_now), jnp.bfloat16)
        .at[place]
        .set(source[tok_index])
    )
    outgoing = buffer.reshape(n_experts, capacity, columns_now)
    gate_local = gate_weight[0]
    up_local = up_weight[0]
    down_local = down_weight[0]
    arrived = lax.all_to_all(outgoing, "expert", split_axis=0, concat_axis=0, tiled=True)
    gate = jnp.einsum("snd,fd->snf", arrived, gate_local, preferred_element_type=jnp.float32)
    up = jnp.einsum("snd,fd->snf", arrived, up_local, preferred_element_type=jnp.float32)
    hidden = (jax.nn.silu(gate) * up).astype(jnp.bfloat16)
    produced = jnp.einsum(
        "snf,fd->snd", hidden, down_local, preferred_element_type=jnp.float32
    ).astype(jnp.bfloat16)
    returned = lax.all_to_all(produced, "expert", split_axis=0, concat_axis=0, tiled=True)
    width = returned.shape[2]
    picked = returned.reshape(n_experts * capacity, width)[place]
    weighted = picked.astype(jnp.float32) * route.reshape(-1)[:, None]
    partial_out = jnp.sum(weighted.reshape(tok_rows, top_count, width), axis=1)
    return lax.psum_scatter(partial_out, "dp", scatter_dimension=1, tiled=True).astype(jnp.bfloat16)


def swap(value, mask):
    n = lax.axis_size("expert")
    return lax.ppermute(value, "expert", [(i, i ^ mask) for i in range(n)])


def swap_dp(value):
    return lax.ppermute(value, "dp", [(0, 1), (1, 0)])


def ffn_kernel(n_blocks, half_ref, *refs):
    xs = refs[:n_blocks]
    w_ref, gate_ref, up_ref, down_ref = refs[n_blocks:n_blocks + 4]
    outs = refs[n_blocks + 4:n_blocks * 2 + 4]
    part = xs[0].shape[2]
    mine = half_ref[0]
    here = [pl.ds(pl.multiple_of((mine if s == 0 else 1 - mine) * part, part), part) for s in range(2)]
    nt = (((1,), (1,)), ((), ()))
    for b in range(n_blocks):
        gate = lax.dot_general(xs[b][0], gate_ref[:, here[0]], nt, preferred_element_type=jnp.float32)
        gate += lax.dot_general(xs[b][1], gate_ref[:, here[1]], nt, preferred_element_type=jnp.float32)
        up = lax.dot_general(xs[b][0], up_ref[:, here[0]], nt, preferred_element_type=jnp.float32)
        up += lax.dot_general(xs[b][1], up_ref[:, here[1]], nt, preferred_element_type=jnp.float32)
        hidden = (gate / (1.0 + jnp.exp(-gate)) * up * w_ref[b]).astype(jnp.bfloat16)
        for s in range(2):
            outs[b][s] = jnp.dot(
                hidden, down_ref[:, here[s]], preferred_element_type=jnp.float32
            ).astype(jnp.bfloat16)


def ffn(xs, weights, gate, up, down, mine):
    n_blocks = len(xs)
    rows, part = xs[0].shape[1:]
    flops = 6 * n_blocks * rows * gate.shape[0] * gate.shape[1]
    vmem = pl.BlockSpec(memory_space=pltpu.VMEM)
    return pl.pallas_call(
        lambda *refs: ffn_kernel(n_blocks, *refs),
        out_shape=[jax.ShapeDtypeStruct((2, rows, part), jnp.bfloat16)] * n_blocks,
        in_specs=[pl.BlockSpec(memory_space=pltpu.SMEM)] + [vmem] * (n_blocks + 4),
        out_specs=[vmem] * n_blocks,
        compiler_params=pltpu.CompilerParams(vmem_limit_bytes=48 * 2**20),
        cost_estimate=pl.CostEstimate(
            flops=flops,
            bytes_accessed=6 * gate.size + 8 * n_blocks * rows * part,
            transcendentals=n_blocks * rows * gate.shape[0],
        ),
        name="ffn",
    )(mine, *xs, weights, gate, up, down)


def gather_all(tokens, expert_ids, chosen_probs, gate_weight, up_weight, down_weight):
    n_experts = lax.axis_size("expert")
    tok_rows, part = tokens.shape
    me = lax.axis_index("expert")
    mine = lax.axis_index("dp").reshape(1).astype(jnp.int32)
    gate, up, down = gate_weight[0], up_weight[0], down_weight[0]

    route = chosen_probs / jnp.sum(chosen_probs, axis=1, keepdims=True)
    chosen = expert_ids.T[None] == jnp.arange(n_experts, dtype=jnp.int32)[:, None, None]
    dense = jnp.sum(jnp.where(chosen, route.T[None], 0.0), axis=1)
    dense = lax.all_to_all(dense, "expert", split_axis=0, concat_axis=0, tiled=True)

    line = [1 << k for k in range(n_experts.bit_length() - 2, 1, -1)]
    step = tok_rows // CHUNKS
    finished = []
    for c in range(CHUNKS):
        masks = [0]
        t = tokens[None, c * step:(c + 1) * step]
        for m in line:
            t = jnp.concatenate([t, swap(t, m)], axis=0)
            masks = masks + [k ^ m for k in masks]
        masks = masks + [k ^ 2 for k in masks]
        n_slots = len(masks)
        a, b = t[:, :step // 2], t[:, step // 2:]
        a = jnp.stack([a, swap_dp(a)])
        b = jnp.concatenate([b, swap(b, 2)], axis=0)
        a = jnp.concatenate([a, swap(a, 2)], axis=1)
        b = jnp.stack([b, swap_dp(b)])
        a = a.reshape(2, n_slots * step // 2, part)
        b = b.reshape(2, n_slots * step // 2, part)
        xs = [a, swap(a, 1), b, swap(b, 1)]
        weights = []
        for p in range(2):
            for core in range(2):
                rows = slice(c * step + p * step // 2, c * step + (p + 1) * step // 2)
                order = me ^ jnp.array([k ^ core for k in masks], jnp.int32)
                weights.append(dense[:, rows][order].reshape(-1, 1))
        outs = ffn(xs, jnp.stack(weights), gate, up, down, mine)
        shape = (2, 2, n_slots // 2, step // 2, part)
        a0, a1, b0, b1 = [o.reshape(shape).astype(jnp.float32) for o in outs]

        def add(keep, got):
            return keep + got.astype(jnp.float32)

        def send(v):
            return v.astype(jnp.bfloat16)

        a = add(a0, swap(send(a1), 1))
        b = add(b0, swap(send(b1), 1))
        a = add(a[:, 0], swap(send(a[:, 1]), 2))
        b = add(b[0], swap_dp(send(b[1])))
        a = add(a[0], swap_dp(send(a[1])))
        b = add(b[0], swap(send(b[1]), 2))
        t = jnp.concatenate([a, b], axis=1)
        for m in reversed(line):
            n = t.shape[0] // 2
            t = add(t[:n], swap(send(t[n:]), m))
        finished.append(t[0].astype(jnp.bfloat16))
    return jnp.concatenate(finished, axis=0)


def solution(mesh):
    n_dp, n_experts = mesh.shape["dp"], mesh.shape["expert"]
    powers = n_experts & (n_experts - 1) == 0
    few = n_dp == 2 and powers and 4 <= n_experts <= 32
    in_specs = (
        P("expert", "dp"),
        P("expert", None),
        P("expert", None),
        P("expert", "dp", None),
        P("expert", "dp", None),
        P("expert", "dp", None),
    )
    return jax.shard_map(
        gather_all if few else exchange,
        mesh=mesh,
        in_specs=in_specs,
        out_specs=P("expert", "dp"),
        check_vma=False,
    )
```

```python
import jax
import jax.numpy as jnp
from jax import lax
from jax.experimental import pallas as pl
from jax.experimental.pallas import tpu as pltpu
from jax.sharding import PartitionSpec as P

VMEM_MB = 40


def exchange(tokens, expert_ids, chosen_probs, gate_weight, up_weight, down_weight):
    n_experts = lax.axis_size("expert")
    tok_rows = expert_ids.shape[0]
    top_count = expert_ids.shape[1]
    capacity = min(
        tok_rows, max(2, (3 * tok_rows * top_count + 2 * n_experts - 1) // (2 * n_experts))
    )
    route = chosen_probs / jnp.sum(chosen_probs, axis=1, keepdims=True)
    flat = expert_ids.reshape(-1)
    onehot = (flat[:, None] == jnp.arange(n_experts, dtype=jnp.int32)[None, :]).astype(jnp.int32)
    slot = jnp.sum(onehot * (jnp.cumsum(onehot, axis=0) - 1), axis=1)
    place = flat * capacity + slot
    tok_index = jnp.arange(tok_rows * top_count, dtype=jnp.int32) // top_count
    source = lax.all_gather(tokens, "dp", axis=1, tiled=True)
    columns_now = source.shape[1]
    buffer = (
        jnp.zeros((n_experts * capacity, columns_now), jnp.bfloat16)
        .at[place]
        .set(source[tok_index])
    )
    outgoing = buffer.reshape(n_experts, capacity, columns_now)
    gate_local = gate_weight[0]
    up_local = up_weight[0]
    down_local = down_weight[0]
    arrived = lax.all_to_all(outgoing, "expert", split_axis=0, concat_axis=0, tiled=True)
    gate = jnp.einsum("snd,fd->snf", arrived, gate_local, preferred_element_type=jnp.float32)
    up = jnp.einsum("snd,fd->snf", arrived, up_local, preferred_element_type=jnp.float32)
    hidden = (jax.nn.silu(gate) * up).astype(jnp.bfloat16)
    produced = jnp.einsum(
        "snf,fd->snd", hidden, down_local, preferred_element_type=jnp.float32
    ).astype(jnp.bfloat16)
    returned = lax.all_to_all(produced, "expert", split_axis=0, concat_axis=0, tiled=True)
    width = returned.shape[2]
    picked = returned.reshape(n_experts * capacity, width)[place]
    weighted = picked.astype(jnp.float32) * route.reshape(-1)[:, None]
    partial_out = jnp.sum(weighted.reshape(tok_rows, top_count, width), axis=1)
    return lax.psum_scatter(partial_out, "dp", scatter_dimension=1, tiled=True).astype(jnp.bfloat16)


def swap(value, mask):
    n = lax.axis_size("expert")
    return lax.ppermute(value, "expert", [(i, i ^ mask) for i in range(n)])


def swap_dp(value):
    return lax.ppermute(value, "dp", [(0, 1), (1, 0)])


def after(value, *events):
    return lax.optimization_barrier((value, *events))[0]


def ffn_kernel(half, z_first, half_ref, *refs):
    pieces = (refs[0:4], refs[4:8])
    w_ref, gate_hbm, up_hbm, down_hbm, own_sent, own_kept = refs[8:14]
    other_sent, other_kept = refs[14:16], refs[16]
    x_scr, gate_ref, up_ref, down_ref, sems = refs[17:]
    rows, part = pieces[0][0].shape[2:]
    lines = pieces[0][0].shape[1]
    ff = gate_ref.shape[0]
    copies = []
    for k, (src, dst) in enumerate(((gate_hbm, gate_ref), (up_hbm, up_ref), (down_hbm, down_ref))):
        for h in range(2):
            at = pl.ds(h * (ff // 2), ff // 2)
            copies.append(pltpu.make_async_copy(src.at[0, at], dst.at[at], sems.at[2 * k + h]))
    for copy in copies:
        copy.start()
    mine = half_ref[0]
    here = [pl.ds(pl.multiple_of((mine if s == 0 else 1 - mine) * part, part), part) for s in range(2)]
    nt = (((1,), (1,)), ((), ()))
    size = lines * rows

    def place(core, y):
        return (core * 2 + y) * size

    for p in range(2):
        for core in range(2):
            for y in range(2):
                for x in range(2):
                    first, second = (y, x) if p == 0 else (x, y)
                    piece = pieces[p][core * 2 + first][second]
                    x_scr[p, x, pl.ds(place(core, y), size), :] = piece.reshape(size, part)

    def project(p, ref):
        return sum(
            lax.dot_general(x_scr[p, s], ref[:, here[s]], nt, preferred_element_type=jnp.float32)
            for s in range(2)
        )

    for p in range(2):
        if p == 0:
            copies[0].wait()
            copies[1].wait()
        gate = project(p, gate_ref)
        if p == 0:
            copies[2].wait()
            copies[3].wait()
        hidden = (gate / (1.0 + jnp.exp(-gate)) * project(p, up_ref)).astype(jnp.bfloat16)
        if p == 0:
            copies[4].wait()
            copies[5].wait()
        for x in range(2):
            out = jnp.dot(hidden, down_ref[:, here[x]], preferred_element_type=jnp.float32)
            for core in range(2):
                for y in range(2):
                    first, second = (y, x) if p == 0 else (x, y)
                    for z in range(lines):
                        at = place(core, y) + z * rows
                        value = out[at:at + rows] * w_ref[core, y, z, 2 * half + p]
                        at = (z, second) if z_first else (second, z)
                        if core and first:
                            other_sent[p][at] = value.astype(jnp.bfloat16)
                        else:
                            ref = other_kept if core else (own_kept, own_sent)[first]
                            ref[(p,) + at] = value.astype(jnp.bfloat16)


def ffn(half, z_first, pieces, weights, gate, up, down, mine):
    rows, part = pieces[0].shape[2:]
    lines = pieces[0].shape[1]
    one = (lines, 2, rows, part) if z_first else (2, lines, rows, part)
    shapes = [(2,) + one, (2,) + one, one, one, (2,) + one]
    n_rows = 4 * lines * rows
    vmem = pl.BlockSpec(memory_space=pltpu.VMEM)
    hbm = pl.BlockSpec(memory_space=pltpu.HBM)
    return pl.pallas_call(
        lambda *refs: ffn_kernel(half, z_first, *refs),
        out_shape=[jax.ShapeDtypeStruct(s, jnp.bfloat16) for s in shapes],
        in_specs=[pl.BlockSpec(memory_space=pltpu.SMEM)] + [vmem] * 9 + [hbm] * 3,
        out_specs=[vmem] * 5,
        scratch_shapes=[
            pltpu.VMEM((2, 2, n_rows, part), jnp.bfloat16),
            pltpu.VMEM(gate.shape[1:], jnp.bfloat16),
            pltpu.VMEM(gate.shape[1:], jnp.bfloat16),
            pltpu.VMEM(gate.shape[1:], jnp.bfloat16),
            pltpu.SemaphoreType.DMA((6,)),
        ],
        compiler_params=pltpu.CompilerParams(vmem_limit_bytes=VMEM_MB * 2**20),
        cost_estimate=pl.CostEstimate(flops=10000000000, bytes_accessed=20000000, transcendentals=0),
        name="ffn",
    )(mine, *pieces, weights, gate, up, down)


def gather_all(tokens, expert_ids, chosen_probs, gate_weight, up_weight, down_weight):
    n_experts = lax.axis_size("expert")
    tok_rows, part = tokens.shape
    me = lax.axis_index("expert")
    mine = lax.axis_index("dp").reshape(1).astype(jnp.int32)
    line = [1 << k for k in range(n_experts.bit_length() - 2, 1, -1)]
    lines = n_experts // 4
    rows = tok_rows // 4
    along = {"x": swap_dp, "y": lambda v: swap(v, 2)}

    def add(keep, got):
        return keep.astype(jnp.float32) + got.astype(jnp.float32)

    def send(v):
        return v.astype(jnp.bfloat16)

    def line_scatter(t):
        for m in reversed(line):
            n = t.shape[0] // 2
            t = add(t[:n], swap(send(t[n:]), m))
        return t[0]

    route = chosen_probs / jnp.sum(chosen_probs, axis=1, keepdims=True)
    chosen = expert_ids.T[None] == jnp.arange(n_experts, dtype=jnp.int32)[:, None, None]
    dense = jnp.sum(jnp.where(chosen, route.T[None], 0.0), axis=1)
    dense = lax.all_to_all(dense, "expert", split_axis=0, concat_axis=0, tiled=True)
    masks = [0]
    for m in line + [2, 1]:
        masks = masks + [k ^ m for k in masks]
    order = me ^ jnp.array(masks, jnp.int32)
    weights = dense[order].reshape(2, 2, lines, 4, rows, 1)

    def spread(v, *events):
        gots = []
        for m in line:
            gots.append(swap(after(v, *events), m))
            v = jnp.concatenate([v, gots[-1]], axis=0)
        a, b = v[None, :, :rows], v[None, :, rows:]
        gots += [along["x"](a), along["y"](b)]
        a = jnp.concatenate([a, gots[-2]], axis=0)
        b = jnp.concatenate([b, gots[-1]], axis=0)
        return (a, along["y"](a)), (b, along["x"](b)), gots

    a, b, gots = spread(tokens[None, :2 * rows])
    c, d, late = spread(tokens[None, 2 * rows:], gots[0])
    a, b = (a[0], after(a[1], weights, *late[-2:])), (b[0], after(b[1], weights, *late[-2:]))

    def run(z_first, a, b, k):
        pieces = []
        for last in (a, b):
            pieces += [*last, *[swap(p, 1) for p in last]]
        return ffn(k, z_first, pieces, weights, gate_weight, up_weight, down_weight, mine)

    def meet(own_sent, other_sent):
        sent = [send(add(own_sent[k], swap(other_sent[k], 1))) for k in range(2)]
        return along["y"](sent[0]), along["x"](sent[1])

    def total(gots, own, other):
        other = swap(other, 1)
        return [add(add(own[k], other[k]), gots[k]) for k in range(2)]

    ab = run(True, a, b, 0)
    ab_gots = meet(ab[0], ab[2:4])
    c, d = [tuple(after(p, ab[0]) for p in v) for v in (c, d)]
    cd = run(False, c, d, 1)
    cd_other = [after(v, *ab_gots) for v in cd[2:4]]
    cd_gots = meet(cd[0], cd_other)
    a, b = total(ab_gots, ab[1], ab[4])
    t = line_scatter(jnp.concatenate([a, b], axis=1))
    a, b = t[:2], t[2:]
    a = add(a[0], along["x"](send(a[1])))
    b = add(b[0], along["y"](send(b[1])))
    c, d = total(cd_gots, cd[1], cd[4])
    c = add(c[0], along["x"](send(c[1])))
    d = add(d[0], along["y"](send(d[1])))
    t = line_scatter(jnp.concatenate([c, d], axis=1))
    return jnp.concatenate([a, b, t], axis=0).astype(jnp.bfloat16)


def solution(mesh):
    n_dp, n_experts = mesh.shape["dp"], mesh.shape["expert"]
    powers = n_experts & (n_experts - 1) == 0
    few = n_dp == 2 and powers and 4 <= n_experts <= 32
    in_specs = (
        P("expert", "dp"),
        P("expert", None),
        P("expert", None),
        P("expert", "dp", None),
        P("expert", "dp", None),
        P("expert", "dp", None),
    )
    return jax.shard_map(
        gather_all if few else exchange,
        mesh=mesh,
        in_specs=in_specs,
        out_specs=P("expert", "dp"),
        check_vma=False,
    )
```

```python
import jax
import jax.numpy as jnp
from jax import lax
from jax.experimental import pallas as pl
from jax.experimental.pallas import tpu as pltpu
from jax.sharding import PartitionSpec as P

VMEM_MB = 40


def exchange(tokens, expert_ids, chosen_probs, gate_weight, up_weight, down_weight):
    n_experts = lax.axis_size("expert")
    tok_rows = expert_ids.shape[0]
    top_count = expert_ids.shape[1]
    capacity = min(
        tok_rows, max(2, (3 * tok_rows * top_count + 2 * n_experts - 1) // (2 * n_experts))
    )
    route = chosen_probs / jnp.sum(chosen_probs, axis=1, keepdims=True)
    flat = expert_ids.reshape(-1)
    onehot = (flat[:, None] == jnp.arange(n_experts, dtype=jnp.int32)[None, :]).astype(jnp.int32)
    slot = jnp.sum(onehot * (jnp.cumsum(onehot, axis=0) - 1), axis=1)
    place = flat * capacity + slot
    tok_index = jnp.arange(tok_rows * top_count, dtype=jnp.int32) // top_count
    source = lax.all_gather(tokens, "dp", axis=1, tiled=True)
    columns_now = source.shape[1]
    buffer = (
        jnp.zeros((n_experts * capacity, columns_now), jnp.bfloat16)
        .at[place]
        .set(source[tok_index])
    )
    outgoing = buffer.reshape(n_experts, capacity, columns_now)
    gate_local = gate_weight[0]
    up_local = up_weight[0]
    down_local = down_weight[0]
    arrived = lax.all_to_all(outgoing, "expert", split_axis=0, concat_axis=0, tiled=True)
    gate = jnp.einsum("snd,fd->snf", arrived, gate_local, preferred_element_type=jnp.float32)
    up = jnp.einsum("snd,fd->snf", arrived, up_local, preferred_element_type=jnp.float32)
    hidden = (jax.nn.silu(gate) * up).astype(jnp.bfloat16)
    produced = jnp.einsum(
        "snf,fd->snd", hidden, down_local, preferred_element_type=jnp.float32
    ).astype(jnp.bfloat16)
    returned = lax.all_to_all(produced, "expert", split_axis=0, concat_axis=0, tiled=True)
    width = returned.shape[2]
    picked = returned.reshape(n_experts * capacity, width)[place]
    weighted = picked.astype(jnp.float32) * route.reshape(-1)[:, None]
    partial_out = jnp.sum(weighted.reshape(tok_rows, top_count, width), axis=1)
    return lax.psum_scatter(partial_out, "dp", scatter_dimension=1, tiled=True).astype(jnp.bfloat16)


def swap(value, mask):
    n = lax.axis_size("expert")
    return lax.ppermute(value, "expert", [(i, i ^ mask) for i in range(n)])


def swap_dp(value):
    return lax.ppermute(value, "dp", [(0, 1), (1, 0)])


def after(value, *events):
    return lax.optimization_barrier((value, *events))[0]


def ffn_kernel(half, z_first, half_ref, *refs):
    pieces = (refs[0:4], refs[4:8])
    w_ref, gate_hbm, up_hbm, down_hbm, own_sent, own_kept = refs[8:14]
    other_sent, other_kept = refs[14:16], refs[16]
    x_scr, gate_ref, up_ref, down_ref, sems = refs[17:]
    rows, part = pieces[0][0].shape[2:]
    lines = pieces[0][0].shape[1]
    ff = gate_ref.shape[0]
    copies = []
    for k, (src, dst) in enumerate(((gate_hbm, gate_ref), (up_hbm, up_ref), (down_hbm, down_ref))):
        for h in range(2):
            at = pl.ds(h * (ff // 2), ff // 2)
            copies.append(pltpu.make_async_copy(src.at[0, at], dst.at[at], sems.at[2 * k + h]))
    for copy in copies:
        copy.start()
    mine = half_ref[0]
    here = [pl.ds(pl.multiple_of((mine if s == 0 else 1 - mine) * part, part), part) for s in range(2)]
    nt = (((1,), (1,)), ((), ()))
    size = lines * rows

    def place(core, y):
        return (core * 2 + y) * size

    for p in range(2):
        for core in range(2):
            for y in range(2):
                for x in range(2):
                    first, second = (y, x) if p == 0 else (x, y)
                    piece = pieces[p][core * 2 + first][second]
                    x_scr[p, x, pl.ds(place(core, y), size), :] = piece.reshape(size, part)

    def project(p, ref):
        return sum(
            lax.dot_general(x_scr[p, s], ref[:, here[s]], nt, preferred_element_type=jnp.float32)
            for s in range(2)
        )

    for p in range(2):
        if p == 0:
            copies[0].wait()
            copies[1].wait()
        gate = project(p, gate_ref)
        if p == 0:
            copies[2].wait()
            copies[3].wait()
        hidden = (gate / (1.0 + jnp.exp(-gate)) * project(p, up_ref)).astype(jnp.bfloat16)
        if p == 0:
            copies[4].wait()
            copies[5].wait()
        for x in range(2):
            out = jnp.dot(hidden, down_ref[:, here[x]], preferred_element_type=jnp.float32)
            for core in range(2):
                for y in range(2):
                    first, second = (y, x) if p == 0 else (x, y)
                    for z in range(lines):
                        at = place(core, y) + z * rows
                        value = out[at:at + rows] * w_ref[core, y, z, 2 * half + p]
                        at = (z, second) if z_first else (second, z)
                        if core and first:
                            other_sent[p][at] = value.astype(jnp.bfloat16)
                        else:
                            ref = other_kept if core else (own_kept, own_sent)[first]
                            ref[(p,) + at] = value.astype(jnp.bfloat16)


def ffn(half, z_first, pieces, weights, gate, up, down, mine):
    rows, part = pieces[0].shape[2:]
    lines = pieces[0].shape[1]
    one = (lines, 2, rows, part) if z_first else (2, lines, rows, part)
    shapes = [(2,) + one, (2,) + one, one, one, (2,) + one]
    n_rows = 4 * lines * rows
    vmem = pl.BlockSpec(memory_space=pltpu.VMEM)
    hbm = pl.BlockSpec(memory_space=pltpu.HBM)
    return pl.pallas_call(
        lambda *refs: ffn_kernel(half, z_first, *refs),
        out_shape=[jax.ShapeDtypeStruct(s, jnp.bfloat16) for s in shapes],
        in_specs=[pl.BlockSpec(memory_space=pltpu.SMEM)] + [vmem] * 9 + [hbm] * 3,
        out_specs=[vmem] * 5,
        scratch_shapes=[
            pltpu.VMEM((2, 2, n_rows, part), jnp.bfloat16),
            pltpu.VMEM(gate.shape[1:], jnp.bfloat16),
            pltpu.VMEM(gate.shape[1:], jnp.bfloat16),
            pltpu.VMEM(gate.shape[1:], jnp.bfloat16),
            pltpu.SemaphoreType.DMA((6,)),
        ],
        compiler_params=pltpu.CompilerParams(vmem_limit_bytes=VMEM_MB * 2**20),
        cost_estimate=pl.CostEstimate(flops=10000000000, bytes_accessed=20000000, transcendentals=0),
        name="ffn",
    )(mine, *pieces, weights, gate, up, down)


def gather_all(tokens, expert_ids, chosen_probs, gate_weight, up_weight, down_weight):
    n_experts = lax.axis_size("expert")
    tok_rows, part = tokens.shape
    me = lax.axis_index("expert")
    mine = lax.axis_index("dp").reshape(1).astype(jnp.int32)
    line = [1 << k for k in range(n_experts.bit_length() - 2, 1, -1)]
    lines = n_experts // 4
    rows = tok_rows // 4
    along = {"x": swap_dp, "y": lambda v: swap(v, 2)}

    def add(keep, got):
        return keep.astype(jnp.float32) + got.astype(jnp.float32)

    def send(v):
        return v.astype(jnp.bfloat16)

    def line_scatter(t):
        for m in reversed(line):
            n = t.shape[0] // 2
            t = add(t[:n], swap(send(t[n:]), m))
        return t[0]

    route = chosen_probs / jnp.sum(chosen_probs, axis=1, keepdims=True)
    chosen = expert_ids.T[None] == jnp.arange(n_experts, dtype=jnp.int32)[:, None, None]
    dense = jnp.sum(jnp.where(chosen, route.T[None], 0.0), axis=1)
    dense = lax.all_to_all(dense, "expert", split_axis=0, concat_axis=0, tiled=True)
    masks = [0]
    for m in line + [2, 1]:
        masks = masks + [k ^ m for k in masks]
    order = me ^ jnp.array(masks, jnp.int32)
    weights = dense[order].reshape(2, 2, lines, 4, rows, 1)

    def spread(v, *events):
        gots = []
        for m in line:
            gots.append(swap(after(v, *events), m))
            v = jnp.concatenate([v, gots[-1]], axis=0)
        if not events:
            v = after(v, weights)
        a, b = v[None, :, :rows], v[None, :, rows:]
        gots += [along["x"](a), along["y"](b)]
        a = jnp.concatenate([a, gots[-2]], axis=0)
        b = jnp.concatenate([b, gots[-1]], axis=0)
        return (a, along["y"](a)), (b, along["x"](b)), gots

    a, b, gots = spread(tokens[None, :2 * rows])
    c, d, late = spread(tokens[None, 2 * rows:], gots[0])
    a, b = (a[0], after(a[1], *late[-2:])), (b[0], after(b[1], *late[-2:]))

    def run(z_first, a, b, k):
        pieces = []
        for last in (a, b):
            pieces += [*last, *[swap(p, 1) for p in last]]
        return ffn(k, z_first, pieces, weights, gate_weight, up_weight, down_weight, mine)

    def meet(own_sent, other_sent):
        sent = [send(add(own_sent[k], swap(other_sent[k], 1))) for k in range(2)]
        return along["y"](sent[0]), along["x"](sent[1])

    def total(gots, own, other):
        other = swap(other, 1)
        return [add(add(own[k], other[k]), gots[k]) for k in range(2)]

    ab = run(True, a, b, 0)
    ab_gots = meet(ab[0], ab[2:4])
    c, d = [tuple(after(p, ab[0]) for p in v) for v in (c, d)]
    cd = run(False, c, d, 1)
    cd_other = [after(v, *ab_gots) for v in cd[2:4]]
    cd_gots = meet(cd[0], cd_other)
    a, b = total(ab_gots, ab[1], ab[4])
    t = line_scatter(jnp.concatenate([a, b], axis=1))
    a, b = t[:2], t[2:]
    a = add(a[0], along["x"](send(a[1])))
    b = add(b[0], along["y"](send(b[1])))
    c, d = total(cd_gots, cd[1], cd[4])
    c = add(c[0], along["x"](send(c[1])))
    d = add(d[0], along["y"](send(d[1])))
    t = line_scatter(jnp.concatenate([c, d], axis=1))
    return jnp.concatenate([a, b, t], axis=0).astype(jnp.bfloat16)


def solution(mesh):
    n_dp, n_experts = mesh.shape["dp"], mesh.shape["expert"]
    powers = n_experts & (n_experts - 1) == 0
    few = n_dp == 2 and powers and 4 <= n_experts <= 32
    in_specs = (
        P("expert", "dp"),
        P("expert", None),
        P("expert", None),
        P("expert", "dp", None),
        P("expert", "dp", None),
        P("expert", "dp", None),
    )
    return jax.shard_map(
        gather_all if few else exchange,
        mesh=mesh,
        in_specs=in_specs,
        out_specs=P("expert", "dp"),
        check_vma=False,
    )
```

```python
import jax
import jax.numpy as jnp
from jax import lax
from jax.experimental import pallas as pl
from jax.experimental.pallas import tpu as pltpu
from jax.sharding import PartitionSpec as P

VMEM_MB = 40


def exchange(tokens, expert_ids, chosen_probs, gate_weight, up_weight, down_weight):
    n_experts = lax.axis_size("expert")
    tok_rows = expert_ids.shape[0]
    top_count = expert_ids.shape[1]
    capacity = min(
        tok_rows, max(2, (3 * tok_rows * top_count + 2 * n_experts - 1) // (2 * n_experts))
    )
    route = chosen_probs / jnp.sum(chosen_probs, axis=1, keepdims=True)
    flat = expert_ids.reshape(-1)
    onehot = (flat[:, None] == jnp.arange(n_experts, dtype=jnp.int32)[None, :]).astype(jnp.int32)
    slot = jnp.sum(onehot * (jnp.cumsum(onehot, axis=0) - 1), axis=1)
    place = flat * capacity + slot
    tok_index = jnp.arange(tok_rows * top_count, dtype=jnp.int32) // top_count
    source = lax.all_gather(tokens, "dp", axis=1, tiled=True)
    columns_now = source.shape[1]
    buffer = (
        jnp.zeros((n_experts * capacity, columns_now), jnp.bfloat16)
        .at[place]
        .set(source[tok_index])
    )
    outgoing = buffer.reshape(n_experts, capacity, columns_now)
    gate_local = gate_weight[0]
    up_local = up_weight[0]
    down_local = down_weight[0]
    arrived = lax.all_to_all(outgoing, "expert", split_axis=0, concat_axis=0, tiled=True)
    gate = jnp.einsum("snd,fd->snf", arrived, gate_local, preferred_element_type=jnp.float32)
    up = jnp.einsum("snd,fd->snf", arrived, up_local, preferred_element_type=jnp.float32)
    hidden = (jax.nn.silu(gate) * up).astype(jnp.bfloat16)
    produced = jnp.einsum(
        "snf,fd->snd", hidden, down_local, preferred_element_type=jnp.float32
    ).astype(jnp.bfloat16)
    returned = lax.all_to_all(produced, "expert", split_axis=0, concat_axis=0, tiled=True)
    width = returned.shape[2]
    picked = returned.reshape(n_experts * capacity, width)[place]
    weighted = picked.astype(jnp.float32) * route.reshape(-1)[:, None]
    partial_out = jnp.sum(weighted.reshape(tok_rows, top_count, width), axis=1)
    return lax.psum_scatter(partial_out, "dp", scatter_dimension=1, tiled=True).astype(jnp.bfloat16)


def swap(value, mask):
    n = lax.axis_size("expert")
    return lax.ppermute(value, "expert", [(i, i ^ mask) for i in range(n)])


def swap_dp(value):
    return lax.ppermute(value, "dp", [(0, 1), (1, 0)])


def after(value, *events):
    return lax.optimization_barrier((value, *events))[0]


def ffn_kernel(half, z_first, half_ref, *refs):
    pieces = (refs[0:4], refs[4:8])
    w_ref, gate_hbm, up_hbm, down_hbm, own_sent, own_kept = refs[8:14]
    other_sent, other_kept = refs[14:16], refs[16]
    x_scr, gate_ref, up_ref, down_ref, sems = refs[17:]
    rows, part = pieces[0][0].shape[2:]
    lines = pieces[0][0].shape[1]
    ff = gate_ref.shape[0]
    copies = []
    for k, (src, dst) in enumerate(((gate_hbm, gate_ref), (up_hbm, up_ref), (down_hbm, down_ref))):
        for h in range(2):
            at = pl.ds(h * (ff // 2), ff // 2)
            copies.append(pltpu.make_async_copy(src.at[0, at], dst.at[at], sems.at[2 * k + h]))
    for copy in copies[:2]:
        copy.start()
    mine = half_ref[0]
    here = [pl.ds(pl.multiple_of((mine if s == 0 else 1 - mine) * part, part), part) for s in range(2)]
    nt = (((1,), (1,)), ((), ()))
    size = lines * rows

    def place(core, y):
        return (core * 2 + y) * size

    for p in range(2):
        for core in range(2):
            for y in range(2):
                for x in range(2):
                    first, second = (y, x) if p == 0 else (x, y)
                    piece = pieces[p][core * 2 + first][second]
                    x_scr[p, x, pl.ds(place(core, y), size), :] = piece.reshape(size, part)

    def project(p, ref):
        return sum(
            lax.dot_general(x_scr[p, s], ref[:, here[s]], nt, preferred_element_type=jnp.float32)
            for s in range(2)
        )

    for p in range(2):
        if p == 0:
            copies[0].wait()
            copies[1].wait()
            for copy in copies[2:]:
                copy.start()
        gate = project(p, gate_ref)
        if p == 0:
            copies[2].wait()
            copies[3].wait()
        hidden = (gate / (1.0 + jnp.exp(-gate)) * project(p, up_ref)).astype(jnp.bfloat16)
        if p == 0:
            copies[4].wait()
            copies[5].wait()
        for x in range(2):
            out = jnp.dot(hidden, down_ref[:, here[x]], preferred_element_type=jnp.float32)
            for core in range(2):
                for y in range(2):
                    first, second = (y, x) if p == 0 else (x, y)
                    for z in range(lines):
                        at = place(core, y) + z * rows
                        value = out[at:at + rows] * w_ref[core, y, z, 2 * half + p]
                        at = (z, second) if z_first else (second, z)
                        if core and first:
                            other_sent[p][at] = value.astype(jnp.bfloat16)
                        else:
                            ref = other_kept if core else (own_kept, own_sent)[first]
                            ref[(p,) + at] = value.astype(jnp.bfloat16)


def ffn(half, z_first, pieces, weights, gate, up, down, mine):
    rows, part = pieces[0].shape[2:]
    lines = pieces[0].shape[1]
    one = (lines, 2, rows, part) if z_first else (2, lines, rows, part)
    shapes = [(2,) + one, (2,) + one, one, one, (2,) + one]
    n_rows = 4 * lines * rows
    vmem = pl.BlockSpec(memory_space=pltpu.VMEM)
    hbm = pl.BlockSpec(memory_space=pltpu.HBM)
    return pl.pallas_call(
        lambda *refs: ffn_kernel(half, z_first, *refs),
        out_shape=[jax.ShapeDtypeStruct(s, jnp.bfloat16) for s in shapes],
        in_specs=[pl.BlockSpec(memory_space=pltpu.SMEM)] + [vmem] * 9 + [hbm] * 3,
        out_specs=[vmem] * 5,
        scratch_shapes=[
            pltpu.VMEM((2, 2, n_rows, part), jnp.bfloat16),
            pltpu.VMEM(gate.shape[1:], jnp.bfloat16),
            pltpu.VMEM(gate.shape[1:], jnp.bfloat16),
            pltpu.VMEM(gate.shape[1:], jnp.bfloat16),
            pltpu.SemaphoreType.DMA((6,)),
        ],
        compiler_params=pltpu.CompilerParams(vmem_limit_bytes=VMEM_MB * 2**20),
        cost_estimate=pl.CostEstimate(flops=10000000000, bytes_accessed=20000000, transcendentals=0),
        name="ffn",
    )(mine, *pieces, weights, gate, up, down)


def gather_all(tokens, expert_ids, chosen_probs, gate_weight, up_weight, down_weight):
    n_experts = lax.axis_size("expert")
    tok_rows, part = tokens.shape
    me = lax.axis_index("expert")
    mine = lax.axis_index("dp").reshape(1).astype(jnp.int32)
    line = [1 << k for k in range(n_experts.bit_length() - 2, 1, -1)]
    lines = n_experts // 4
    rows = tok_rows // 4
    along = {"x": swap_dp, "y": lambda v: swap(v, 2)}

    def add(keep, got):
        return keep.astype(jnp.float32) + got.astype(jnp.float32)

    def send(v):
        return v.astype(jnp.bfloat16)

    def line_scatter(t):
        for m in reversed(line):
            n = t.shape[0] // 2
            t = add(t[:n], swap(send(t[n:]), m))
        return t[0]

    route = chosen_probs / jnp.sum(chosen_probs, axis=1, keepdims=True)
    chosen = expert_ids.T[None] == jnp.arange(n_experts, dtype=jnp.int32)[:, None, None]
    dense = jnp.sum(jnp.where(chosen, route.T[None], 0.0), axis=1)
    dense = lax.all_to_all(dense, "expert", split_axis=0, concat_axis=0, tiled=True)
    masks = [0]
    for m in line + [2, 1]:
        masks = masks + [k ^ m for k in masks]
    order = me ^ jnp.array(masks, jnp.int32)
    weights = dense[order].reshape(2, 2, lines, 4, rows, 1)

    def spread(v, *events):
        gots = []
        for m in line:
            gots.append(swap(after(v, *events), m))
            v = jnp.concatenate([v, gots[-1]], axis=0)
        if not events:
            v = after(v, weights)
        a, b = v[None, :, :rows], v[None, :, rows:]
        gots += [along["x"](a), along["y"](b)]
        a = jnp.concatenate([a, gots[-2]], axis=0)
        b = jnp.concatenate([b, gots[-1]], axis=0)
        a, b = lax.optimization_barrier((a, b))
        return (a, along["y"](a)), (b, along["x"](b)), gots

    a, b, gots = spread(tokens[None, :2 * rows])
    c, d, late = spread(tokens[None, 2 * rows:], gots[0])
    a, b = (a[0], after(a[1], *late[-2:])), (b[0], after(b[1], *late[-2:]))

    def run(z_first, a, b, k):
        pieces = []
        for last in (a, b):
            pieces += [*last, *[swap(p, 1) for p in last]]
        return ffn(k, z_first, pieces, weights, gate_weight, up_weight, down_weight, mine)

    def meet(own_sent, other_sent):
        sent = [send(add(own_sent[k], swap(other_sent[k], 1))) for k in range(2)]
        return along["y"](sent[0]), along["x"](sent[1])

    def total(gots, own, other):
        other = swap(other, 1)
        return [add(add(own[k], other[k]), gots[k]) for k in range(2)]

    ab = run(True, a, b, 0)
    ab_gots = meet(ab[0], ab[2:4])
    c, d = [tuple(after(p, ab[0]) for p in v) for v in (c, d)]
    cd = run(False, c, d, 1)
    cd_other = [after(v, *ab_gots) for v in cd[2:4]]
    cd_gots = meet(cd[0], cd_other)
    a, b = total(ab_gots, ab[1], ab[4])
    t = line_scatter(jnp.concatenate([a, b], axis=1))
    a, b = t[:2], t[2:]
    a = add(a[0], along["x"](send(a[1])))
    b = add(b[0], along["y"](send(b[1])))
    c, d = total(cd_gots, cd[1], cd[4])
    c = add(c[0], along["x"](send(c[1])))
    d = add(d[0], along["y"](send(d[1])))
    t = line_scatter(jnp.concatenate([c, d], axis=1))
    return jnp.concatenate([a, b, t], axis=0).astype(jnp.bfloat16)


def solution(mesh):
    n_dp, n_experts = mesh.shape["dp"], mesh.shape["expert"]
    powers = n_experts & (n_experts - 1) == 0
    few = n_dp == 2 and powers and 4 <= n_experts <= 32
    in_specs = (
        P("expert", "dp"),
        P("expert", None),
        P("expert", None),
        P("expert", "dp", None),
        P("expert", "dp", None),
        P("expert", "dp", None),
    )
    return jax.shard_map(
        gather_all if few else exchange,
        mesh=mesh,
        in_specs=in_specs,
        out_specs=P("expert", "dp"),
        check_vma=False,
    )
```
